32 devices in a mesh: seq: 8 (over y, x, core), ch: 4 (over z).
Axes of the slice: x: 2, y: 2, z: 4, core: 2. Of those that a mesh axis runs over, the one named last changes fastest.
Arguments:
- tokens: bfloat16 [65536, 512], P('seq', 'ch'), may hold values from -6 to 6
- gate: bfloat16 [65536, 512], P('seq', 'ch'), may hold values from -6 to 6
- cotangent: bfloat16 [65536, 512], P('seq', 'ch'), may hold values from -6 to 6
- w_first: bfloat16 [1024, 1024], replicated, may hold values from -0.1875 to 0.1875
- w_second: bfloat16 [64, 64], replicated, may hold values from -0.75 to 0.75
Outputs:
- mixed: bfloat16 [65536, 512], P('seq', 'ch')
- grad_tokens: bfloat16 [65536, 512], P('seq', 'ch')
- grad_gate: bfloat16 [65536, 512], P('seq', 'ch')
- grad_first: float32 [1024, 1024], replicated
- grad_second: float32 [64, 64], replicated
The draws below stay inside these ranges and needn't reach their ends.
All inputs are finite; a program needn't handle non-finite values.
Results may differ from the reference program's by a relative error of at most 0.0058.
Values may be sent and summed in bfloat16 or wider, within the bound.
A program may use at most 128 MiB of HBM per device.

```python
import jax
import jax.numpy as jnp

BLK = 1024
C = 512
NB = 64
TOKENS = 65536


def block_levels(stream_key, shape, cuts, smallest, top_value):
    factor_of, own = 1.0, jax.random.fold_in(stream_key, 6)
    for position, parts in cuts:
        steps = jnp.exp(jax.random.uniform(jax.random.fold_in(own, position), (parts,), jnp.float32, smallest / len(cuts), top_value / len(cuts)))
        factor_of = factor_of * jnp.repeat(steps, shape[position] // parts).reshape([-1 if axis == position else 1 for axis in range(len(shape))])
    return factor_of


def normal_values(rng, extent, width, bound, split=(), dtype=jnp.bfloat16):
    drawn = width * jax.random.normal(rng, extent, jnp.float32)
    if split:
        drawn = drawn * block_levels(rng, extent, split, -0.22, 0.18)
    return jnp.clip(drawn, -bound, bound).astype(dtype)


def setup_inputs(seed: int = 0) -> dict:
    key_of = jax.random.split(jax.random.key(seed), 6)
    return {
        "tokens": normal_values(key_of[0], (TOKENS, C), 1.0, 6.0, ((0, 8), (1, 4))),
        "gate": normal_values(key_of[1], (TOKENS, C), 1.5, 6.0, ((0, 8), (1, 4))),
        "cotangent": normal_values(key_of[2], (TOKENS, C), 1.0, 6.0, ((0, 8), (1, 4))),
        "w_first": normal_values(key_of[3], (BLK, BLK), BLK ** -0.5, 0.1875),
        "w_second": normal_values(key_of[4], (NB, NB), NB ** -0.5, 0.75),
    }


def reference(tokens, gate, cotangent, w_first, w_second):
    x = tokens.reshape(NB, BLK, C)
    g = gate.reshape(NB, BLK, C).astype(jnp.float32)
    dz = cotangent.reshape(NB, BLK, C).astype(jnp.float32)
    w1 = w_first.astype(jnp.float32)
    w2 = w_second.astype(jnp.float32)
    first = jnp.einsum('jk,ikc->ijc', w1, x.astype(jnp.float32))
    sig = jax.nn.sigmoid(g)
    act = g * sig
    slope = sig * (1.0 + g * (1.0 - sig))
    hidden = (first * act).astype(jnp.bfloat16)
    hidden32 = hidden.astype(jnp.float32)
    mixed = jnp.einsum('il,ljc->ijc', w2, hidden32).astype(jnp.bfloat16)
    grad_hidden = jnp.einsum('il,ijc->ljc', w2, dz).astype(jnp.bfloat16)
    grad_second = jnp.einsum('ijc,ljc->il', dz, hidden32) / jnp.sqrt(jnp.float32(BLK * C))
    gh32 = grad_hidden.astype(jnp.float32)
    grad_first_act = (gh32 * act).astype(jnp.bfloat16)
    grad_gate = (gh32 * first * slope).astype(jnp.bfloat16)
    gfa32 = grad_first_act.astype(jnp.float32)
    grad_tokens = jnp.einsum('jk,ijc->ikc', w1, gfa32).astype(jnp.bfloat16)
    grad_first = jnp.einsum('ijc,ikc->jk', gfa32, x.astype(jnp.float32)) / jnp.sqrt(jnp.float32(NB * C))
    return (mixed.reshape(TOKENS, C), grad_tokens.reshape(TOKENS, C), grad_gate.reshape(TOKENS, C), grad_first, grad_second)
```

```python
import functools

import jax
import jax.numpy as jnp
from jax import lax
from jax.experimental import pallas as pl
from jax.experimental.pallas import tpu as pltpu
from jax.sharding import PartitionSpec as P

MESH = pl.DeviceIdType.MESH
BF = jnp.bfloat16
F32 = jnp.float32
GRP = 16
CHUNKS = 2
NT = (((1,), (1,)), ((), ()))
TN = (((0,), (0,)), ((), ()))


def dot(a, b, dims=(((1,), (0,)), ((), ()))):
    return lax.dot_general(a, b, dims, preferred_element_type=F32)


def loop(lo, hi, body):
    def step(i, carry):
        body(i)
        return carry

    lax.fori_loop(lo, hi, step, 0)


def remote(src, dst, send, recv, dev):
    return pltpu.make_async_remote_copy(
        src_ref=src, dst_ref=dst, send_sem=send, recv_sem=recv, device_id=dev, device_id_type=MESH
    )


def fused(ns, nch, lb, pp, width,
          x_hbm, g_hbm, dz_hbm, w1_hbm, w2_ref,
          mixed_hbm, gt_hbm, gg_hbm, gf_hbm, gs_ref,
          xv, gv, w1v, wk, wkt, act, fs, hid, dzt, ht, ght, ghr, mt, gfa, gtv,
          pf, pb, r1, s1b, r2, s2, s2b, r3, gfo, gsr, gsr2,
          ld, dz_l, mx_l, out_l,
          dz_s, dz_r, gh_s, gh_r, h_s, h_r, mx_s, mx_r,
          a1_s, a1_r, a2_s, a2_r, a3_s, a3_r, b3_s, b3_r, b2_s, b2_r, b1_s, b1_r,
          q_s, q_r, q2_s, q2_r):
    nc = CHUNKS
    pc = pp // nc
    block = ns * pp
    nb = lb * ns
    big = nb * GRP
    me = lax.axis_index("seq")
    zz = lax.axis_index("ch")
    core = lax.rem(me, 2)
    quad = me // 2
    nq = ns // 2
    half = block // nc // 2
    zrows = half // nch
    qrows = zrows // nq

    def peer(d):
        return lax.rem(me + d, ns)

    def zpeer(d):
        return lax.rem(zz + d, nch)

    def qpeer(d):
        return lax.rem(quad + d, nq)

    loads = [
        pltpu.make_async_copy(w1_hbm, w1v, ld.at[0]),
        pltpu.make_async_copy(x_hbm, xv, ld.at[1]),
        pltpu.make_async_copy(g_hbm, gv, ld.at[2]),
    ]
    dz_own = [
        pltpu.make_async_copy(dz_hbm.at[:, me, h], dzt.at[h, pl.ds(me * lb, lb)], dz_l.at[h])
        for h in range(nc)
    ]
    for c in loads:
        c.start()
    for c in dz_own:
        c.start()

    barrier = pltpu.get_barrier_semaphore()
    loop(1, ns, lambda d: pl.semaphore_signal(barrier, inc=1, device_id={"seq": peer(d)}, device_id_type=MESH))
    loop(1, nch, lambda d: pl.semaphore_signal(barrier, inc=1, device_id={"ch": zpeer(d)}, device_id_type=MESH))
    pl.semaphore_wait(barrier, ns + nch - 2)

    mine = pl.ds(me * lb, lb)

    def dz_copy(h, d):
        return remote(dz_hbm.at[:, peer(d), h], dzt.at[h, mine], dz_s.at[h, d], dz_r.at[h, d], {"seq": peer(d)})

    def gh_copy(h, d):
        return remote(ght.at[h, pl.ds(peer(d) * lb, lb)], ghr.at[h, me], gh_s.at[h, d], gh_r.at[h, d], {"seq": peer(d)})

    def h_copy(h, d):
        return remote(hid.at[:, peer(d), h], ht.at[h, mine], h_s.at[h, d], h_r.at[h, d], {"seq": peer(d)})

    def mx_copy(h, d):
        return remote(mt.at[h, pl.ds(peer(d) * lb, lb)], mixed_hbm.at[:, me, h], mx_s.at[h, d], mx_r.at[h, d], {"seq": peer(d)})

    def start(f, h, n):
        loop(1, n, lambda d: f(h, d).start())

    def recv(f, h, n):
        loop(1, n, lambda d: f(h, d).wait_recv())

    def sent(f, h, n):
        loop(1, n, lambda d: f(h, d).wait_send())

    for h in range(nc):
        start(dz_copy, h, ns)

    tile = 256

    def onehot(rows, cols, first_row):
        r = lax.broadcasted_iota(jnp.int32, (rows, cols), 0) + first_row
        c = lax.broadcasted_iota(jnp.int32, (rows, cols), 1)
        return jnp.where(r // GRP == c, 1.0, 0.0).astype(F32)

    def same(rows, cols):
        r = lax.broadcasted_iota(jnp.int32, (rows, cols), 0)
        c = lax.broadcasted_iota(jnp.int32, (rows, cols), 1)
        return r % GRP == c % GRP

    def expand(t):
        rows = pl.ds(pl.multiple_of(t * tile, tile), tile)
        e = onehot(tile, nb, t * tile).astype(BF)
        every = onehot(big, nb, 0).astype(BF)
        keep = same(tile, big)
        w2 = w2_ref[...]
        wk[rows, :] = jnp.where(keep, dot(dot(e, w2).astype(BF), every, NT), 0.0).astype(BF)
        wkt[rows, :] = jnp.where(keep, dot(dot(e, w2, NT).astype(BF), every, NT), 0.0).astype(BF)

    loop(0, big // tile, expand)

    for c in loads:
        c.wait()

    def forward(i):
        b = jnp.concatenate(
            [xv[2 * i].reshape(block, width), xv[2 * i + 1].reshape(block, width)], axis=1
        )
        f2 = dot(w1v[...], b)
        for s in range(2):
            f = f2[:, s * width : (s + 1) * width]
            g = gv[2 * i + s].reshape(block, width).astype(F32)
            sig = 1.0 / (1.0 + jnp.exp(-g))
            a = g * sig
            shape = (ns, nc, pc, width)
            act[2 * i + s] = a.reshape(shape)
            fs[2 * i + s] = (f * (sig * (1.0 + g * (1.0 - sig)))).reshape(shape)
            hid[2 * i + s] = (f * a).astype(BF).reshape(shape)

    loop(0, lb // 2, forward)

    def pair(ref, h, q, rows):
        lo = pl.multiple_of(q * 2 * GRP, 2 * GRP)
        hi = pl.multiple_of(lo + GRP, GRP)
        n = rows.size * GRP
        return jnp.concatenate(
            [ref[h, rows, pl.ds(lo, GRP), :].reshape(n, width), ref[h, rows, pl.ds(hi, GRP), :].reshape(n, width)],
            axis=1,
        )

    def mix(w_ref, src, dst, h):
        def body(q):
            lo = pl.multiple_of(q * 2 * GRP, 2 * GRP)
            hi = pl.multiple_of(lo + GRP, GRP)
            out = dot(w_ref[...], pair(src, h, q, pl.ds(0, nb))).astype(BF)
            dst[h, :, pl.ds(lo, GRP), :] = out[:, :width].reshape(nb, GRP, width)
            dst[h, :, pl.ds(hi, GRP), :] = out[:, width:].reshape(nb, GRP, width)

        loop(0, pc // (2 * GRP), body)

    for h in range(nc):
        dz_own[h].wait()
        recv(dz_copy, h, ns)
        mix(wkt, dzt, ght, h)
        start(gh_copy, h, ns)
        ghr[h, me] = ght[h, mine]

    def a1(h):
        return remote(pb.at[h, pl.ds((1 - core) * half, half)], r1.at[h], a1_s.at[h], a1_r.at[h], {"seq": me + 1 - 2 * core})

    def a2(h, d):
        return remote(s1b.at[h, pl.ds(zpeer(d) * zrows, zrows)], r2.at[h, d], a2_s.at[h, d], a2_r.at[h, d], {"ch": zpeer(d)})

    def a3(h, d):
        return remote(s2b.at[h, pl.ds(qpeer(d) * qrows, qrows)], r3.at[h, d], a3_s.at[h, d], a3_r.at[h, d], {"seq": qpeer(d) * 2 + core})

    def b3(h, d):
        part = gfo.at[h, pl.ds(core * half + zz * zrows + quad * qrows, qrows)]
        return remote(part, part, b3_s.at[h, d], b3_r.at[h, d], {"seq": qpeer(d) * 2 + core})

    def b2(h, d):
        part = gfo.at[h, pl.ds(core * half + zz * zrows, zrows)]
        return remote(part, part, b2_s.at[h, d], b2_r.at[h, d], {"ch": zpeer(d)})

    def b1(h):
        part = gfo.at[h, pl.ds(core * half, half)]
        return remote(part, part, b1_s.at[h], b1_r.at[h], {"seq": me + 1 - 2 * core})

    per = tile // pp

    def term(h):
        def gates(p):
            gh = ghr[h, p].astype(F32)
            gfa[:, p, h] = (gh * act[:, p, h]).astype(BF)
            gv[:, p, h] = (gh * fs[:, p, h]).astype(BF)

        loop(0, ns, gates)

        def cols(t):
            acc = None
            for i in range(0, lb, 2):
                a = jnp.concatenate(
                    [gfa[i + s, :, h].reshape(ns * pc, width) for s in range(2)], axis=1
                )
                b = jnp.concatenate(
                    [xv[i + s, pl.ds(t * per, per)].reshape(tile, width) for s in range(2)], axis=1
                )
                v = dot(a, b, NT)
                acc = v if acc is None else acc + v
            where = pl.ds(pl.multiple_of(t * tile, tile), tile)
            pf[h, :, where] = acc
            pb[h, :, where] = acc.astype(BF)

        loop(0, block // tile, cols)

    for h in range(nc):
        recv(gh_copy, h, ns)
        start(h_copy, h, ns)
        ht[h, mine] = hid[:, me, h]
        term(h)
        a1(h).start()

    for h in range(nc):
        a1(h).wait_recv()
        low = pl.ds(pl.multiple_of(core * half, half), half)
        total = pf[h, low, :] + r1[h].astype(F32)
        pf[h, low, :] = total
        s1b[h] = total.astype(BF)
        start(a2, h, nch)

    out_gg = pltpu.make_async_copy(gv, gg_hbm, out_l.at[0])
    out_gg.start()

    def tokens(i):
        b = jnp.concatenate(
            [gfa[2 * i].reshape(block, width), gfa[2 * i + 1].reshape(block, width)], axis=1
        )
        out = dot(w1v[...], b, TN).astype(BF)
        for s in range(2):
            gtv[2 * i + s] = out[:, s * width : (s + 1) * width].reshape(ns, nc, pc, width)

    loop(0, lb // 2, tokens)
    out_gt = pltpu.make_async_copy(gtv, gt_hbm, out_l.at[1])
    out_gt.start()

    mx_own = [
        pltpu.make_async_copy(mt.at[h, mine], mixed_hbm.at[:, me, h], mx_l.at[h]) for h in range(nc)
    ]
    for h in range(nc):
        recv(h_copy, h, ns)
        mix(wk, ht, mt, h)
        start(mx_copy, h, ns)
        mx_own[h].start()

    for h in range(nc):
        recv(a2, h, nch)
        low = pl.multiple_of(core * half + zz * zrows, zrows)
        total = pf[h, pl.ds(low, zrows), :]
        for d in range(1, nch):
            total = total + r2[h, d].astype(F32)
        s2[h] = total
        s2b[h] = total.astype(BF)
        start(a3, h, nq)

    def second(t):
        rows = pl.ds(t * (tile // GRP), tile // GRP)
        acc = None
        for h in range(nc):
            for q in range(pc // (2 * GRP)):
                v = dot(pair(dzt, h, q, rows), pair(ht, h, q, pl.ds(0, nb)), NT)
                acc = v if acc is None else acc + v
        acc = jnp.where(same(tile, big), acc, 0.0)
        acc = acc.reshape(tile // GRP, GRP, big).sum(axis=1)
        gsr[me, pl.ds(pl.multiple_of(t * (tile // GRP), tile // GRP), tile // GRP), :] = lax.dot_general(
            acc, onehot(big, 128, 0), (((1,), (0,)), ((), ())),
            precision=lax.Precision.HIGHEST, preferred_element_type=F32,
        )

    loop(0, big // tile, second)

    def q1(h, d):
        return remote(gsr.at[me], gsr.at[me], q_s.at[d], q_r.at[d], {"seq": peer(d)})

    def q2(h, d):
        return remote(gsr2.at[zz], gsr2.at[zz], q2_s.at[d], q2_r.at[d], {"ch": zpeer(d)})

    start(q1, 0, ns)

    for h in range(nc):
        recv(a3, h, nq)
        total = s2[h, pl.ds(pl.multiple_of(quad * qrows, qrows), qrows), :]
        for d in range(1, nq):
            total = total + r3[h, d].astype(F32)
        gfo[h, pl.ds(pl.multiple_of(core * half + zz * zrows + quad * qrows, qrows), qrows), :] = total.astype(BF)
        start(b3, h, nq)

    for h in range(nc):
        recv(b3, h, nq)
        sent(b3, h, nq)
        start(b2, h, nch)

    recv(q1, 0, ns)
    sent(q1, 0, ns)
    total = gsr[0]
    for d in range(1, ns):
        total = total + gsr[d]
    gsr2[zz] = total
    start(q2, 0, nch)

    for h in range(nc):
        recv(b2, h, nch)
        sent(b2, h, nch)
        b1(h).start()

    recv(q2, 0, nch)
    sent(q2, 0, nch)
    total = gsr2[0]
    for d in range(1, nch):
        total = total + gsr2[d]
    gs_ref[...] = total

    for h in range(nc):
        b1(h).wait_recv()
        b1(h).wait_send()
    out_gf = pltpu.make_async_copy(gfo, gf_hbm, out_l.at[2])
    out_gf.start()

    for h in range(nc):
        sent(dz_copy, h, ns)
        sent(gh_copy, h, ns)
        sent(h_copy, h, ns)
        a1(h).wait_send()
        sent(a2, h, nch)
        sent(a3, h, nq)
    for h in range(nc):
        mx_own[h].wait()
        recv(mx_copy, h, ns)
        sent(mx_copy, h, ns)
    out_gg.wait()
    out_gt.wait()
    out_gf.wait()


def local_fused(tokens, gate, cotangent, w_first, w_second):
    ns = lax.axis_size("seq")
    nch = lax.axis_size("ch")
    width = tokens.shape[1]
    block = w_first.shape[0]
    lb = tokens.shape[0] // block
    nb = lb * ns
    pp = block // ns
    nc = CHUNKS
    pc = pp // nc
    nq = ns // 2
    half = block // nc // 2
    zrows = half // nch
    qrows = zrows // nq
    big = nb * GRP
    five = (lb, ns, nc, pc, width)
    spread = (nc, nb, pc, width)
    anyspec = pl.BlockSpec(memory_space=pl.ANY)
    vmem = pl.BlockSpec(memory_space=pltpu.VMEM)
    V = pltpu.VMEM
    D = pltpu.SemaphoreType.DMA
    scratch = [
        V(five, BF), V(five, BF), V((block, block), BF), V((big, big), BF), V((big, big), BF),
        V(five, F32), V(five, F32), V(five, BF),
        V(spread, BF), V(spread, BF), V(spread, BF), V((nc, ns, lb, pc, width), BF), V(spread, BF),
        V(five, BF), V(five, BF),
        V((nc, 2 * half, block), F32), V((nc, 2 * half, block), BF),
        V((nc, half, block), BF), V((nc, half, block), BF),
        V((nc, nch, zrows, block), BF), V((nc, zrows, block), F32), V((nc, zrows, block), BF),
        V((nc, nq, qrows, block), BF), V((nc, 2 * half, block), BF),
        V((ns, nb, 128), F32), V((nch, nb, 128), F32),
        D((3,)), D((nc,)), D((nc,)), D((3,)),
    ]
    scratch += [D((nc, ns))] * 8
    scratch += [D((nc,))] * 2 + [D((nc, nch))] * 2 + [D((nc, nq))] * 4 + [D((nc, nch))] * 2 + [D((nc,))] * 2
    scratch += [D((ns,))] * 2 + [D((nch,))] * 2
    sd = jax.ShapeDtypeStruct
    mixed, gt, gg, gf, gs = pl.pallas_call(
        functools.partial(fused, ns, nch, lb, pp, width),
        out_shape=(sd(five, BF), sd(five, BF), sd(five, BF), sd((nc, 2 * half, block), BF), sd((nb, 128), F32)),
        in_specs=[anyspec] * 4 + [vmem],
        out_specs=(anyspec, anyspec, anyspec, anyspec, vmem),
        scratch_shapes=scratch,
        compiler_params=pltpu.CompilerParams(
            collective_id=0, has_side_effects=True, vmem_limit_bytes=60 * 1024 * 1024
        ),
        name="fused",
    )(tokens.reshape(five), gate.reshape(five), cotangent.reshape(five), w_first, w_second)
    total_width = width * nch
    gf = gf.reshape(nc, ns, pc, block).transpose(1, 0, 2, 3).reshape(block, block)
    grad_first = gf.astype(F32) / jnp.sqrt(F32(nb * total_width))
    grad_second = gs[:, :nb] / jnp.sqrt(F32(block * total_width))
    return mixed.reshape(tokens.shape), gt.reshape(tokens.shape), gg.reshape(tokens.shape), grad_first, grad_second


def local(tokens, gate, cotangent, w_first, w_second):
    seq_count = lax.axis_size("seq")
    chan_count = lax.axis_size("ch")
    width = tokens.shape[1]
    block = w_first.shape[0]
    local_blocks = tokens.shape[0] // block
    all_blocks = local_blocks * seq_count
    x_blocks = tokens.reshape(local_blocks, block, width)
    gate_f = gate.reshape(local_blocks, block, width).astype(jnp.float32)
    cot_blocks = cotangent.reshape(local_blocks, block, width)
    first = jnp.einsum("jk,ikc->ijc", w_first, x_blocks, preferred_element_type=jnp.float32)
    sig = jax.nn.sigmoid(gate_f)
    act = gate_f * sig
    slope = sig * (1.0 + gate_f * (1.0 - sig))
    hidden = (first * act).astype(jnp.bfloat16)
    hidden_t = lax.all_to_all(hidden, "seq", split_axis=1, concat_axis=0, tiled=True)
    mixed_t = jnp.einsum(
        "il,ljc->ijc", w_second, hidden_t, preferred_element_type=jnp.float32
    ).astype(jnp.bfloat16)
    mixed = lax.all_to_all(mixed_t, "seq", split_axis=0, concat_axis=1, tiled=True)
    cot_t = lax.all_to_all(cot_blocks, "seq", split_axis=1, concat_axis=0, tiled=True)
    grad_hidden_t = jnp.einsum(
        "il,ijc->ljc", w_second, cot_t, preferred_element_type=jnp.float32
    ).astype(jnp.bfloat16)
    grad_hidden = lax.all_to_all(grad_hidden_t, "seq", split_axis=0, concat_axis=1, tiled=True)
    second_term = jnp.einsum("ijc,ljc->il", cot_t, hidden_t, preferred_element_type=jnp.float32)
    gh_float = grad_hidden.astype(jnp.float32)
    grad_first_act = (gh_float * act).astype(jnp.bfloat16)
    grad_gate = (gh_float * first * slope).astype(jnp.bfloat16)
    grad_tokens = jnp.einsum(
        "jk,ijc->ikc", w_first, grad_first_act, preferred_element_type=jnp.float32
    ).astype(jnp.bfloat16)
    first_term = jnp.einsum(
        "ijc,ikc->jk", grad_first_act, x_blocks, preferred_element_type=jnp.float32
    )
    first_sum, second_sum = lax.psum((first_term, second_term), ("seq", "ch"))
    total_width = width * chan_count
    grad_first = first_sum / jnp.sqrt(jnp.float32(all_blocks * total_width))
    grad_second = second_sum / jnp.sqrt(jnp.float32(block * total_width))
    rows = local_blocks * block
    return (
        mixed.reshape(rows, width),
        grad_tokens.reshape(rows, width),
        grad_gate.reshape(rows, width),
        grad_first,
        grad_second,
    )


def fits(mesh, tokens, w_first):
    ns, nch = mesh.shape["seq"], mesh.shape["ch"]
    block = w_first.shape[0]
    width = tokens.shape[1] // nch
    lb = tokens.shape[0] // ns // block
    pp = block // ns
    if width != 128 or lb % 2 or ns % 2 or lb * ns * GRP > 1024 or (lb * ns * GRP) % 256:
        return False
    if block > 1024 or block % 256 or 256 % pp or pp % (CHUNKS * 2 * GRP):
        return False
    return (block // CHUNKS) % (ns * nch * GRP) == 0 and lb * ns <= 128 and lb <= 8


def solution(mesh):
    def run(tokens, gate, cotangent, w_first, w_second):
        return jax.shard_map(
            local_fused if fits(mesh, tokens, w_first) else local,
            mesh=mesh,
            in_specs=(P("seq", "ch"), P("seq", "ch"), P("seq", "ch"), P(), P()),
            out_specs=(P("seq", "ch"), P("seq", "ch"), P("seq", "ch"), P(), P()),
            check_vma=False,
        )(tokens, gate, cotangent, w_first, w_second)

    return run
```

```python
import functools

import jax
import jax.numpy as jnp
from jax import lax
from jax.experimental import pallas as pl
from jax.experimental.pallas import tpu as pltpu
from jax.sharding import PartitionSpec as P

MESH = pl.DeviceIdType.MESH
BF = jnp.bfloat16
F32 = jnp.float32
GRP = 16
CHUNKS = 2
NT = (((1,), (1,)), ((), ()))
TN = (((0,), (0,)), ((), ()))


def dot(a, b, dims=(((1,), (0,)), ((), ()))):
    return lax.dot_general(a, b, dims, preferred_element_type=F32)


def loop(lo, hi, body):
    def step(i, carry):
        body(i)
        return carry

    lax.fori_loop(lo, hi, step, 0)


def remote(src, dst, send, recv, dev):
    return pltpu.make_async_remote_copy(
        src_ref=src, dst_ref=dst, send_sem=send, recv_sem=recv, device_id=dev, device_id_type=MESH
    )


def fused(ns, nch, lb, pp, width,
          x_hbm, g_hbm, dz_hbm, w1_hbm, w2_ref,
          mixed_hbm, gt_hbm, gg_hbm, gf_hbm, gs_ref,
          xv, gv, w1v, wk, wkt, act, fs, hid, dzt, ht, ght, ghr, mt, gfa, gtv,
          pf, pb, r1, s1b, r2, s2, s2b, r3, gfo, gsr, gsr2,
          ld, dz_l, mx_l, out_l, gf_l,
          dz_s, dz_r, gh_s, gh_r, h_s, h_r, mx_s, mx_r,
          a1_s, a1_r, a2_s, a2_r, a3_s, a3_r, b3_s, b3_r, b2_s, b2_r, b1_s, b1_r,
          q_s, q_r, q2_s, q2_r):
    nc = CHUNKS
    pc = pp // nc
    block = ns * pp
    nb = lb * ns
    big = nb * GRP
    me = lax.axis_index("seq")
    zz = lax.axis_index("ch")
    core = lax.rem(me, 2)
    quad = me // 2
    nq = ns // 2
    half = block // nc // 2
    zrows = half // nch
    qrows = zrows // nq

    def peer(d):
        return lax.rem(me + d, ns)

    def zpeer(d):
        return lax.rem(zz + d, nch)

    def qpeer(d):
        return lax.rem(quad + d, nq)

    loads = [
        pltpu.make_async_copy(w1_hbm, w1v, ld.at[0]),
        pltpu.make_async_copy(x_hbm, xv, ld.at[1]),
        pltpu.make_async_copy(g_hbm, gv, ld.at[2]),
    ]
    dz_own = [
        pltpu.make_async_copy(dz_hbm.at[:, me, h], dzt.at[h, pl.ds(me * lb, lb)], dz_l.at[h])
        for h in range(nc)
    ]
    for c in loads:
        c.start()
    for c in dz_own:
        c.start()

    barrier = pltpu.get_barrier_semaphore()
    loop(1, ns, lambda d: pl.semaphore_signal(barrier, inc=1, device_id={"seq": peer(d)}, device_id_type=MESH))
    loop(1, nch, lambda d: pl.semaphore_signal(barrier, inc=1, device_id={"ch": zpeer(d)}, device_id_type=MESH))
    pl.semaphore_wait(barrier, ns + nch - 2)

    mine = pl.ds(me * lb, lb)

    def dz_copy(h, d):
        return remote(dz_hbm.at[:, peer(d), h], dzt.at[h, mine], dz_s.at[h, d], dz_r.at[h, d], {"seq": peer(d)})

    def gh_copy(h, d):
        return remote(ght.at[h, pl.ds(peer(d) * lb, lb)], ghr.at[h, me], gh_s.at[h, d], gh_r.at[h, d], {"seq": peer(d)})

    def h_copy(h, d):
        return remote(hid.at[:, peer(d), h], ht.at[h, mine], h_s.at[h, d], h_r.at[h, d], {"seq": peer(d)})

    def mx_copy(h, d):
        return remote(mt.at[h, pl.ds(peer(d) * lb, lb)], mixed_hbm.at[:, me, h], mx_s.at[h, d], mx_r.at[h, d], {"seq": peer(d)})

    def start(f, h, n):
        loop(1, n, lambda d: f(h, d).start())

    def recv(f, h, n):
        loop(1, n, lambda d: f(h, d).wait_recv())

    def sent(f, h, n):
        loop(1, n, lambda d: f(h, d).wait_send())

    for h in range(nc):
        start(dz_copy, h, ns)

    tile = 256

    def onehot(rows, cols, first_row):
        r = lax.broadcasted_iota(jnp.int32, (rows, cols), 0) + first_row
        c = lax.broadcasted_iota(jnp.int32, (rows, cols), 1)
        return jnp.where(r // GRP == c, 1.0, 0.0).astype(F32)

    def same(rows, cols):
        r = lax.broadcasted_iota(jnp.int32, (rows, cols), 0)
        c = lax.broadcasted_iota(jnp.int32, (rows, cols), 1)
        return r % GRP == c % GRP

    def expand(t):
        rows = pl.ds(pl.multiple_of(t * tile, tile), tile)
        e = onehot(tile, nb, t * tile).astype(BF)
        every = onehot(big, nb, 0).astype(BF)
        keep = same(tile, big)
        w2 = w2_ref[...]
        wk[rows, :] = jnp.where(keep, dot(dot(e, w2).astype(BF), every, NT), 0.0).astype(BF)
        wkt[rows, :] = jnp.where(keep, dot(dot(e, w2, NT).astype(BF), every, NT), 0.0).astype(BF)

    loop(0, big // tile, expand)

    for c in loads:
        c.wait()

    def forward(i):
        b = jnp.concatenate(
            [xv[2 * i].reshape(block, width), xv[2 * i + 1].reshape(block, width)], axis=1
        )
        f2 = dot(w1v[...], b)
        for s in range(2):
            f = f2[:, s * width : (s + 1) * width]
            g = gv[2 * i + s].reshape(block, width).astype(F32)
            sig = 1.0 / (1.0 + jnp.exp(-g))
            a = g * sig
            shape = (ns, nc, pc, width)
            act[2 * i + s] = a.reshape(shape)
            fs[2 * i + s] = (f * (sig * (1.0 + g * (1.0 - sig)))).reshape(shape)
            hid[2 * i + s] = (f * a).astype(BF).reshape(shape)

    loop(0, lb // 2, forward)

    def pair(ref, h, q, rows):
        lo = pl.multiple_of(q * 2 * GRP, 2 * GRP)
        hi = pl.multiple_of(lo + GRP, GRP)
        n = rows.size * GRP
        return jnp.concatenate(
            [ref[h, rows, pl.ds(lo, GRP), :].reshape(n, width), ref[h, rows, pl.ds(hi, GRP), :].reshape(n, width)],
            axis=1,
        )

    def mix(w_ref, src, dst, h):
        def body(q):
            lo = pl.multiple_of(q * 2 * GRP, 2 * GRP)
            hi = pl.multiple_of(lo + GRP, GRP)
            out = dot(w_ref[...], pair(src, h, q, pl.ds(0, nb))).astype(BF)
            dst[h, :, pl.ds(lo, GRP), :] = out[:, :width].reshape(nb, GRP, width)
            dst[h, :, pl.ds(hi, GRP), :] = out[:, width:].reshape(nb, GRP, width)

        loop(0, pc // (2 * GRP), body)

    for h in range(nc):
        dz_own[h].wait()
        recv(dz_copy, h, ns)
        mix(wkt, dzt, ght, h)
        start(gh_copy, h, ns)
        ghr[h, me] = ght[h, mine]

    def a1(h):
        return remote(pb.at[h, pl.ds((1 - core) * half, half)], r1.at[h], a1_s.at[h], a1_r.at[h], {"seq": me + 1 - 2 * core})

    def a2(h, d):
        return remote(s1b.at[h, pl.ds(zpeer(d) * zrows, zrows)], r2.at[h, d], a2_s.at[h, d], a2_r.at[h, d], {"ch": zpeer(d)})

    def a3(h, d):
        return remote(s2b.at[h, pl.ds(qpeer(d) * qrows, qrows)], r3.at[h, d], a3_s.at[h, d], a3_r.at[h, d], {"seq": qpeer(d) * 2 + core})

    def b3(h, d):
        part = gfo.at[h, pl.ds(core * half + zz * zrows + quad * qrows, qrows)]
        return remote(part, part, b3_s.at[h, d], b3_r.at[h, d], {"seq": qpeer(d) * 2 + core})

    def b2(h, d):
        part = gfo.at[h, pl.ds(core * half + zz * zrows, zrows)]
        return remote(part, part, b2_s.at[h, d], b2_r.at[h, d], {"ch": zpeer(d)})

    def b1(h):
        part = gfo.at[h, pl.ds(core * half, half)]
        return remote(part, part, b1_s.at[h], b1_r.at[h], {"seq": me + 1 - 2 * core})

    per = tile // pp

    def term(h):
        def gates(p):
            gh = ghr[h, p].astype(F32)
            gfa[:, p, h] = (gh * act[:, p, h]).astype(BF)
            gv[:, p, h] = (gh * fs[:, p, h]).astype(BF)

        loop(0, ns, gates)

        def cols(t):
            acc = None
            for i in range(0, lb, 2):
                a = jnp.concatenate(
                    [gfa[i + s, :, h].reshape(ns * pc, width) for s in range(2)], axis=1
                )
                b = jnp.concatenate(
                    [xv[i + s, pl.ds(t * per, per)].reshape(tile, width) for s in range(2)], axis=1
                )
                v = dot(a, b, NT)
                acc = v if acc is None else acc + v
            where = pl.ds(pl.multiple_of(t * tile, tile), tile)
            pf[h, :, where] = acc
            pb[h, :, where] = acc.astype(BF)

        loop(0, block // tile, cols)

    for h in range(nc):
        recv(gh_copy, h, ns)
        start(h_copy, h, ns)
        ht[h, mine] = hid[:, me, h]
        term(h)
        a1(h).start()

    for h in range(nc):
        a1(h).wait_recv()
        low = pl.ds(pl.multiple_of(core * half, half), half)
        total = pf[h, low, :] + r1[h].astype(F32)
        pf[h, low, :] = total
        s1b[h] = total.astype(BF)
        start(a2, h, nch)

    out_gg = pltpu.make_async_copy(gv, gg_hbm, out_l.at[0])
    out_gg.start()

    def tokens(i):
        b = jnp.concatenate(
            [gfa[2 * i].reshape(block, width), gfa[2 * i + 1].reshape(block, width)], axis=1
        )
        out = dot(w1v[...], b, TN).astype(BF)
        for s in range(2):
            gtv[2 * i + s] = out[:, s * width : (s + 1) * width].reshape(ns, nc, pc, width)

    loop(0, lb // 2, tokens)
    out_gt = pltpu.make_async_copy(gtv, gt_hbm, out_l.at[1])
    out_gt.start()

    for h in range(nc):
        recv(a2, h, nch)
        low = pl.multiple_of(core * half + zz * zrows, zrows)
        total = pf[h, pl.ds(low, zrows), :]
        for d in range(1, nch):
            total = total + r2[h, d].astype(F32)
        s2[h] = total
        s2b[h] = total.astype(BF)
        start(a3, h, nq)

    for h in range(nc):
        recv(a3, h, nq)
        total = s2[h, pl.ds(pl.multiple_of(quad * qrows, qrows), qrows), :]
        for d in range(1, nq):
            total = total + r3[h, d].astype(F32)
        gfo[h, pl.ds(pl.multiple_of(core * half + zz * zrows + quad * qrows, qrows), qrows), :] = total.astype(BF)
        start(b3, h, nq)

    mx_own = [
        pltpu.make_async_copy(mt.at[h, mine], mixed_hbm.at[:, me, h], mx_l.at[h]) for h in range(nc)
    ]
    for h in range(nc):
        if h == nc - 1:
            for e in range(nc):
                recv(b3, e, nq)
                sent(b3, e, nq)
                start(b2, e, nch)
        recv(h_copy, h, ns)
        mix(wk, ht, mt, h)
        start(mx_copy, h, ns)
        mx_own[h].start()

    def second(t):
        rows = pl.ds(t * (tile // GRP), tile // GRP)
        acc = None
        for h in range(nc):
            for q in range(pc // (2 * GRP)):
                v = dot(pair(dzt, h, q, rows), pair(ht, h, q, pl.ds(0, nb)), NT)
                acc = v if acc is None else acc + v
        acc = jnp.where(same(tile, big), acc, 0.0)
        acc = acc.reshape(tile // GRP, GRP, big).sum(axis=1)
        gsr[me, pl.ds(pl.multiple_of(t * (tile // GRP), tile // GRP), tile // GRP), :] = lax.dot_general(
            acc, onehot(big, 128, 0), (((1,), (0,)), ((), ())),
            precision=lax.Precision.HIGHEST, preferred_element_type=F32,
        )

    loop(0, big // tile, second)

    def q1(h, d):
        return remote(gsr.at[me], gsr.at[me], q_s.at[d], q_r.at[d], {"seq": peer(d)})

    def q2(h, d):
        return remote(gsr2.at[zz], gsr2.at[zz], q2_s.at[d], q2_r.at[d], {"ch": zpeer(d)})

    start(q1, 0, ns)

    recv(q1, 0, ns)
    sent(q1, 0, ns)
    total = gsr[0]
    for d in range(1, ns):
        total = total + gsr[d]
    gsr2[zz] = total
    start(q2, 0, nch)

    for h in range(nc):
        recv(b2, h, nch)
        sent(b2, h, nch)
        b1(h).start()

    recv(q2, 0, nch)
    sent(q2, 0, nch)
    total = gsr2[0]
    for d in range(1, nch):
        total = total + gsr2[d]
    gs_ref[...] = total[:, :nb] / jnp.sqrt(F32(block * width * nch))

    for h in range(nc):
        b1(h).wait_recv()
        b1(h).wait_send()
    def out_gf(h, p):
        rows = pl.ds(pl.multiple_of(p * pc, pc), pc)
        return pltpu.make_async_copy(gfo.at[h, rows], gf_hbm.at[p, h], gf_l.at[h, p])

    for h in range(nc):
        loop(0, ns, lambda p: out_gf(h, p).start())

    for h in range(nc):
        sent(dz_copy, h, ns)
        sent(gh_copy, h, ns)
        sent(h_copy, h, ns)
        a1(h).wait_send()
        sent(a2, h, nch)
        sent(a3, h, nq)
    for h in range(nc):
        mx_own[h].wait()
        recv(mx_copy, h, ns)
        sent(mx_copy, h, ns)
    out_gg.wait()
    out_gt.wait()
    for h in range(nc):
        loop(0, ns, lambda p: out_gf(h, p).wait())


def finish(terms, mixed, gt, gg, gf, gs, mixed_out, gt_out, gg_out, gf_out, gs_out):
    mixed_out[...] = mixed[...]
    gt_out[...] = gt[...]
    gg_out[...] = gg[...]
    gf_out[...] = gf[...].astype(F32) / jnp.sqrt(F32(terms))
    gs_out[...] = gs[...]


def local_fused(tokens, gate, cotangent, w_first, w_second):
    ns = lax.axis_size("seq")
    nch = lax.axis_size("ch")
    width = tokens.shape[1]
    block = w_first.shape[0]
    lb = tokens.shape[0] // block
    nb = lb * ns
    pp = block // ns
    nc = CHUNKS
    pc = pp // nc
    nq = ns // 2
    half = block // nc // 2
    zrows = half // nch
    qrows = zrows // nq
    big = nb * GRP
    five = (lb, ns, nc, pc, width)
    spread = (nc, nb, pc, width)
    anyspec = pl.BlockSpec(memory_space=pl.ANY)
    vmem = pl.BlockSpec(memory_space=pltpu.VMEM)
    V = pltpu.VMEM
    D = pltpu.SemaphoreType.DMA
    scratch = [
        V(five, BF), V(five, BF), V((block, block), BF), V((big, big), BF), V((big, big), BF),
        V(five, F32), V(five, F32), V(five, BF),
        V(spread, BF), V(spread, BF), V(spread, BF), V((nc, ns, lb, pc, width), BF), V(spread, BF),
        V(five, BF), V(five, BF),
        V((nc, 2 * half, block), F32), V((nc, 2 * half, block), BF),
        V((nc, half, block), BF), V((nc, half, block), BF),
        V((nc, nch, zrows, block), BF), V((nc, zrows, block), F32), V((nc, zrows, block), BF),
        V((nc, nq, qrows, block), BF), V((nc, 2 * half, block), BF),
        V((ns, nb, 128), F32), V((nch, nb, 128), F32),
        D((3,)), D((nc,)), D((nc,)), D((2,)), D((nc, ns)),
    ]
    scratch += [D((nc, ns))] * 8
    scratch += [D((nc,))] * 2 + [D((nc, nch))] * 2 + [D((nc, nq))] * 4 + [D((nc, nch))] * 2 + [D((nc,))] * 2
    scratch += [D((ns,))] * 2 + [D((nch,))] * 2
    sd = jax.ShapeDtypeStruct
    mixed, gt, gg, gf, gs = pl.pallas_call(
        functools.partial(fused, ns, nch, lb, pp, width),
        out_shape=(sd(five, BF), sd(five, BF), sd(five, BF), sd((ns, nc, pc, block), BF), sd((nb, nb), F32)),
        in_specs=[anyspec] * 4 + [vmem],
        out_specs=(anyspec, anyspec, anyspec, anyspec, vmem),
        scratch_shapes=scratch,
        compiler_params=pltpu.CompilerParams(
            collective_id=0, has_side_effects=True, vmem_limit_bytes=60 * 1024 * 1024
        ),
        name="fused",
    )(tokens.reshape(five), gate.reshape(five), cotangent.reshape(five), w_first, w_second)
    total_width = width * nch
    rows, cells = pl.BlockSpec((block, width), lambda i: (i, 0)), pl.BlockSpec((block // lb, block), lambda i: (i, 0))
    return pl.pallas_call(
        functools.partial(finish, nb * width * nch),
        grid=(lb,),
        out_shape=(sd(tokens.shape, BF),) * 3 + (sd((block, block), F32), sd((nb, nb), F32)),
        in_specs=[rows] * 3 + [cells, vmem],
        out_specs=(rows, rows, rows, cells, pl.BlockSpec((nb, nb), lambda i: (0, 0))),
        name="finish",
    )(mixed.reshape(tokens.shape), gt.reshape(tokens.shape), gg.reshape(tokens.shape), gf.reshape(block, block), gs)


def local(tokens, gate, cotangent, w_first, w_second):
    seq_count = lax.axis_size("seq")
    chan_count = lax.axis_size("ch")
    width = tokens.shape[1]
    block = w_first.shape[0]
    local_blocks = tokens.shape[0] // block
    all_blocks = local_blocks * seq_count
    x_blocks = tokens.reshape(local_blocks, block, width)
    gate_f = gate.reshape(local_blocks, block, width).astype(jnp.float32)
    cot_blocks = cotangent.reshape(local_blocks, block, width)
    first = jnp.einsum("jk,ikc->ijc", w_first, x_blocks, preferred_element_type=jnp.float32)
    sig = jax.nn.sigmoid(gate_f)
    act = gate_f * sig
    slope = sig * (1.0 + gate_f * (1.0 - sig))
    hidden = (first * act).astype(jnp.bfloat16)
    hidden_t = lax.all_to_all(hidden, "seq", split_axis=1, concat_axis=0, tiled=True)
    mixed_t = jnp.einsum(
        "il,ljc->ijc", w_second, hidden_t, preferred_element_type=jnp.float32
    ).astype(jnp.bfloat16)
    mixed = lax.all_to_all(mixed_t, "seq", split_axis=0, concat_axis=1, tiled=True)
    cot_t = lax.all_to_all(cot_blocks, "seq", split_axis=1, concat_axis=0, tiled=True)
    grad_hidden_t = jnp.einsum(
        "il,ijc->ljc", w_second, cot_t, preferred_element_type=jnp.float32
    ).astype(jnp.bfloat16)
    grad_hidden = lax.all_to_all(grad_hidden_t, "seq", split_axis=0, concat_axis=1, tiled=True)
    second_term = jnp.einsum("ijc,ljc->il", cot_t, hidden_t, preferred_element_type=jnp.float32)
    gh_float = grad_hidden.astype(jnp.float32)
    grad_first_act = (gh_float * act).astype(jnp.bfloat16)
    grad_gate = (gh_float * first * slope).astype(jnp.bfloat16)
    grad_tokens = jnp.einsum(
        "jk,ijc->ikc", w_first, grad_first_act, preferred_element_type=jnp.float32
    ).astype(jnp.bfloat16)
    first_term = jnp.einsum(
        "ijc,ikc->jk", grad_first_act, x_blocks, preferred_element_type=jnp.float32
    )
    first_sum, second_sum = lax.psum((first_term, second_term), ("seq", "ch"))
    total_width = width * chan_count
    grad_first = first_sum / jnp.sqrt(jnp.float32(all_blocks * total_width))
    grad_second = second_sum / jnp.sqrt(jnp.float32(block * total_width))
    rows = local_blocks * block
    return (
        mixed.reshape(rows, width),
        grad_tokens.reshape(rows, width),
        grad_gate.reshape(rows, width),
        grad_first,
        grad_second,
    )


def fits(mesh, tokens, w_first):
    ns, nch = mesh.shape["seq"], mesh.shape["ch"]
    block = w_first.shape[0]
    width = tokens.shape[1] // nch
    lb = tokens.shape[0] // ns // block
    pp = block // ns
    if width != 128 or lb % 2 or ns % 2 or lb * ns * GRP > 1024 or (lb * ns * GRP) % 256:
        return False
    if block > 1024 or block % 256 or block % (lb * GRP) or 256 % pp or pp % (CHUNKS * 2 * GRP):
        return False
    return (block // CHUNKS) % (ns * nch * GRP) == 0 and lb * ns <= 128 and lb <= 8


def solution(mesh):
    def run(tokens, gate, cotangent, w_first, w_second):
        return jax.shard_map(
            local_fused if fits(mesh, tokens, w_first) else local,
            mesh=mesh,
            in_specs=(P("seq", "ch"), P("seq", "ch"), P("seq", "ch"), P(), P()),
            out_specs=(P("seq", "ch"), P("seq", "ch"), P("seq", "ch"), P(), P()),
            check_vma=False,
        )(tokens, gate, cotangent, w_first, w_second)

    return run
```
